256 devices in a mesh: row: 8 (over z_lo, core), col: 32 (over y, x, z_hi).
Axes of the slice: x: 4, y: 4, z: 8 (z_hi: 2, z_lo: 4; z = z_hi * 4 + z_lo), core: 2. Of those that a mesh axis runs over, the one named last changes fastest.
Arguments:
- pair: bfloat16 [32, 8, 2, 512, 128], P(None, 'row', None, 'col'), may hold values from -5 to 5
- w_query: bfloat16 [2, 2, 128, 256], replicated, may hold values from -4 to 4
- w_key: bfloat16 [2, 2, 128, 256], replicated, may hold values from -4 to 4
- w_value: bfloat16 [2, 2, 128, 256], replicated, may hold values from -0.5 to 0.5
- w_gate: bfloat16 [2, 2, 128, 256], replicated, may hold values from -0.5 to 0.5
- w_out: bfloat16 [2, 2, 256, 128], replicated, may hold values from -3 to 3
- w_in: bfloat16 [2, 128, 512], replicated, may hold values from -0.5 to 0.5
- w_back: bfloat16 [2, 512, 128], replicated, may hold values from -0.25 to 0.25
Outputs:
- pair_out: bfloat16 [32, 8, 2, 512, 128], P(None, 'row', None, 'col')
The draws below stay inside these ranges and needn't reach their ends.
All inputs are finite; a program needn't handle non-finite values.
Results may differ from the reference program's by a relative error of at most 0.03.
Values may be sent and summed in bfloat16 or wider, within the bound.
A program may use at most 64 MiB of HBM per device.

```python
from functools import partial
import jax
import jax.numpy as jnp
from jax import lax

CHANNELS = 128
HEADS = 8
HEAD_DIM = 32
FF_UNITS = 512
LAYERS = 2
SPAN = 2
GROUPS = 8
BLOCKS = 32
RESIDUES = 512
INNER = 256


def draw_pair(key, part):
    full_grid = jax.random.normal(jax.random.fold_in(key, 11), (RESIDUES, RESIDUES, CHANNELS), jnp.float32)
    full_grid = jnp.clip(full_grid, -5.0, 5.0)
    return full_grid.reshape(BLOCKS, GROUPS, SPAN, RESIDUES, CHANNELS).astype(jnp.bfloat16)


def query_key_pair(key):
    full_shape = (LAYERS, 2, CHANNELS, HEADS, HEAD_DIM)
    spread = CHANNELS ** (-0.5)
    first_draw = jax.random.normal(jax.random.fold_in(key, 21), full_shape, jnp.float32) * spread
    second_draw = jax.random.normal(jax.random.fold_in(key, 22), full_shape, jnp.float32) * spread
    first_draw = jnp.clip(first_draw, -4.0, 4.0).reshape(LAYERS, 2, CHANNELS, HEADS * HEAD_DIM)
    second_draw = jnp.clip(second_draw, -4.0, 4.0).reshape(LAYERS, 2, CHANNELS, HEADS * HEAD_DIM)
    return (first_draw, second_draw)


def draw_w_query(key, part):
    return query_key_pair(key)[0].astype(jnp.bfloat16)


def draw_w_key(key, part):
    return query_key_pair(key)[1].astype(jnp.bfloat16)


def normal_values(own_key, extent, scale, bound, dtype=jnp.bfloat16):
    array = scale * jax.random.normal(own_key, extent, jnp.float32)
    return jnp.clip(array, min=-bound, max=bound).astype(dtype)


def setup_inputs(seed: int = 0) -> dict:
    seeds = jax.random.split(jax.random.key(seed), 9)
    pair = draw_pair(jax.random.fold_in(seeds[8], 71), 0)
    w_query = draw_w_query(jax.random.fold_in(seeds[8], 71), 0)
    w_key = draw_w_key(jax.random.fold_in(seeds[8], 71), 0)
    w_value = normal_values(seeds[3], (LAYERS, 2, CHANNELS, INNER), CHANNELS ** -0.5, 0.5)
    w_gate = normal_values(seeds[4], (LAYERS, 2, CHANNELS, INNER), CHANNELS ** -0.5, 0.5)
    w_out = normal_values(seeds[5], (LAYERS, 2, INNER, CHANNELS), 0.5, 3.0)
    w_in = normal_values(seeds[6], (LAYERS, CHANNELS, FF_UNITS), CHANNELS ** -0.5, 0.5)
    w_back = normal_values(seeds[7], (LAYERS, FF_UNITS, CHANNELS), FF_UNITS ** -0.5, 0.25)
    return dict(pair=pair, w_query=w_query, w_key=w_key, w_value=w_value, w_gate=w_gate, w_out=w_out, w_in=w_in, w_back=w_back)


epsilon = 1e-05

def rounded(values):
    return lax.optimization_barrier(values.astype(jnp.bfloat16))

def layer_norm(values):
    wide = values.astype(jnp.float32)
    center = wide - lax.optimization_barrier(jnp.mean(wide, axis=-1, keepdims=True))
    spread = lax.optimization_barrier(jnp.mean(center * center, axis=-1, keepdims=True))
    return rounded(center * lax.rsqrt(spread + epsilon))

def split_heads(matrix):
    return matrix.reshape(matrix.shape[0], HEADS, matrix.shape[1] // HEADS).astype(jnp.float32)

def one_row(normed, weights):
    wide = normed.astype(jnp.float32)
    queries = rounded(jnp.einsum('qc,chd->hqd', wide, split_heads(weights[0])))
    key_rows = rounded(jnp.einsum('qc,chd->hqd', wide, split_heads(weights[1])))
    value_rows = rounded(jnp.einsum('qc,chd->hqd', wide, split_heads(weights[2])))
    gating = jax.nn.sigmoid(jnp.einsum('qc,chd->hqd', wide, split_heads(weights[3])))
    scores = jnp.einsum('hqd,hkd->hqk', queries.astype(jnp.float32), key_rows.astype(jnp.float32)) * HEAD_DIM ** (-0.5)
    maximum = lax.optimization_barrier(jnp.max(scores, axis=-1, keepdims=True))
    exponent = jnp.exp(scores - maximum)
    denominator = lax.optimization_barrier(jnp.sum(exponent, axis=-1, keepdims=True))
    probs = rounded(exponent)
    blended = jnp.einsum('hqk,hkd->hqd', probs.astype(jnp.float32), value_rows.astype(jnp.float32)) / denominator
    gated_out = rounded(gating * blended)
    out_heads = weights[4].reshape(HEADS, HEAD_DIM, CHANNELS).astype(jnp.float32)
    return jnp.einsum('hqd,hdc->qc', gated_out.astype(jnp.float32), out_heads)

def attend_rows(grid, weights):
    normed = layer_norm(grid)
    update = lax.map(partial(one_row, weights=weights), normed)
    return rounded(grid.astype(jnp.float32) + update)

def reference(pair, w_query, w_key, w_value, w_gate, w_out, w_in, w_back):
    grid = pair.reshape(RESIDUES, RESIDUES, CHANNELS)

    def layer_step(grid, layer_weights):
        row_mats = tuple((matrix[0] for matrix in layer_weights[:5]))
        col_mats = tuple((matrix[1] for matrix in layer_weights[:5]))
        grid = attend_rows(grid, row_mats)
        flipped = jnp.swapaxes(grid, 0, 1)
        grid = jnp.swapaxes(attend_rows(flipped, col_mats), 0, 1)
        symmetric = rounded(0.5 * (grid.astype(jnp.float32) + jnp.swapaxes(grid, 0, 1).astype(jnp.float32)))
        normed = layer_norm(symmetric).reshape(RESIDUES * RESIDUES, CHANNELS)
        hidden = rounded(jax.nn.relu(jnp.dot(normed, layer_weights[5], preferred_element_type=jnp.float32)))
        ff_out = jnp.dot(hidden, layer_weights[6], preferred_element_type=jnp.float32)
        flat = symmetric.reshape(RESIDUES * RESIDUES, CHANNELS).astype(jnp.float32)
        grid = rounded(flat + ff_out).reshape(RESIDUES, RESIDUES, CHANNELS)
        return (grid, None)
    final_grid, unused = lax.scan(layer_step, grid, (w_query, w_key, w_value, w_gate, w_out, w_in, w_back))
    return final_grid.reshape(pair.shape)
```

```python
import math

import jax
import jax.numpy as jnp
from jax import lax
from jax.experimental import pallas as pl
from jax.experimental.pallas import tpu as pltpu
from jax.sharding import PartitionSpec as P

HEADS = 8
HEAD_DIM = 32
INNER = HEADS * HEAD_DIM
CHANNELS = 128
FF = 512
LENGTH = 512
EPSILON = 1e-05
SCALE = math.log2(math.e) / math.sqrt(HEAD_DIM)
MESH = pl.DeviceIdType.MESH
BF = jnp.bfloat16
F32 = jnp.float32
NT = (((1,), (1,)), ((), ()))
TN = (((0,), (0,)), ((), ()))


def layer_norm(wide):
    center = wide - jnp.mean(wide, axis=-1, keepdims=True)
    spread = jnp.mean(center * center, axis=-1, keepdims=True)
    return (center * lax.rsqrt(spread + EPSILON)).astype(BF)


def kernel(
    x, w_query, w_key, w_value, w_gate, w_out, w_in, w_back, out,
    wqt, wvt, wgt, qt, kr, vt, gt, go, grid, mix,
    zr, zc, a_send, a_recv, b_send, b_recv,
    send_sem, in_sem, a_sem, b_sem, t_sem, m_sem,
):
    r = lax.axis_index("row")
    c = lax.axis_index("col")
    core = r % 2
    zl = r // 2
    zv = (zl + 2) % 4
    cy = c // 8
    cx = (c // 2) % 4
    zh = c % 2
    ga = cx * 2 + core
    gb = zv * 8 + cy * 2 + zh
    rd = zv * 2 + core

    def peer_a(g):
        return (zl * 2 + g % 2, cy * 8 + (g // 2) * 2 + zh)

    def peer_b(g):
        return (((g // 8 + 2) % 4) * 2 + core, ((g // 2) % 4) * 8 + cx * 2 + g % 2)

    def copy(src, dst, sem, device):
        return pltpu.make_async_remote_copy(src, dst, send_sem, sem, device_id=device, device_id_type=MESH)

    def loop(start, stop, body):
        lax.fori_loop(start, stop, lambda k, carry: (body(k), carry)[1], 0)

    barrier = pltpu.get_barrier_semaphore()
    loop(0, 32, lambda k: pl.semaphore_signal(barrier, inc=1, device_id=(rd, k), device_id_type=MESH))
    loop(1, 8, lambda k: pl.semaphore_signal(barrier, inc=1, device_id=((r + k) % 8, c), device_id_type=MESH))
    pl.semaphore_wait(barrier, 39)

    place = pl.multiple_of((cx * 8 + cy * 2 + zh) * 16, 16)
    for e in range(2):

        def send_rows(k):
            d = (c + k) % 32
            copy(x.at[d, e], zr.at[e, pl.ds(place, 16)], in_sem.at[e], (rd, d)).start()

        loop(0, 32, send_rows)

    for l in range(2):
        for n in range(2):
            for source, target in ((w_query, wqt), (w_value, wvt), (w_gate, wgt)):
                target[l, n] = source[l, n].astype(F32).T.astype(BF)
    vt[...] = jnp.ones_like(vt)

    def attend(values, l, n):
        wide = values.astype(F32)
        normed = layer_norm(wide)
        qt[...] = (lax.dot_general(wqt[l, n], normed, NT, preferred_element_type=F32) * SCALE).astype(BF)
        kr[...] = jnp.dot(normed, w_key[l, n], preferred_element_type=F32).astype(BF)
        value_rows = lax.dot_general(wvt[l, n], normed, NT, preferred_element_type=F32).astype(BF)
        for h in range(HEADS):
            vt[h, 0:HEAD_DIM, :] = value_rows[h * HEAD_DIM : (h + 1) * HEAD_DIM]
        gt[...] = jax.nn.sigmoid(lax.dot_general(wgt[l, n], normed, NT, preferred_element_type=F32))

        def scores_of(h):
            rows = slice(h * HEAD_DIM, (h + 1) * HEAD_DIM)
            return jnp.dot(kr[:, rows], qt[rows, :], preferred_element_type=F32)

        def probs_of(scores):
            return jnp.exp2(scores - jnp.max(scores, axis=0, keepdims=True)).astype(BF)

        def blend(h, probs):
            rows = slice(h * HEAD_DIM, (h + 1) * HEAD_DIM)
            total = jnp.dot(vt[h], probs, preferred_element_type=F32)
            go[rows, :] = (gt[rows, :] * total[:HEAD_DIM] / total[HEAD_DIM : HEAD_DIM + 1]).astype(BF)

        scores = scores_of(0)
        probs = None
        for h in range(HEADS):
            later = scores_of(h + 1) if h + 1 < HEADS else None
            fresh = probs_of(scores)
            if probs is not None:
                blend(h - 1, probs)
            probs, scores = fresh, later
        blend(HEADS - 1, probs)
        return wide + lax.dot_general(go[...], w_out[l, n], TN, preferred_element_type=F32)

    def transition(wide, l):
        normed = layer_norm(wide)
        hidden = jax.nn.relu(jnp.dot(normed, w_in[l], preferred_element_type=F32)).astype(BF)
        return (wide + jnp.dot(hidden, w_back[l], preferred_element_type=F32)).astype(BF)

    def send_a(ex, e, first_order):
        for g in range(8):
            for t in range(2):
                if first_order:
                    start = (g // 2) * 128 + (g % 2) * 2 + t
                    part = jnp.concatenate(
                        [grid[pl.ds(start + 4 * q, 8, stride=16), :] for q in range(4)], axis=0
                    )
                else:
                    part = grid[pl.ds(g * 2 + t, 32, stride=16), :]
                a_send[ex, g, e, t * 32 : t * 32 + 32, :] = part.astype(BF)

        def go_a(k):
            g = (ga + k) % 8
            copy(a_send.at[ex, g, e], a_recv.at[ex, ga, e], a_sem.at[ex, e], peer_a(g)).start()

        loop(1, 8, go_a)
        a_recv[ex, ga, e] = a_send[ex, ga, e]

    def send_b(ex):
        for e in range(2):
            copy(a_recv.at[ex, pl.ds(0, 7), e], a_recv.at[ex, pl.ds(0, 7), e], a_sem.at[ex, e], (rd, c)).wait_recv()
        for t in range(2):
            for g in range(8):
                for e in range(2):
                    mix[pl.ds(t * 512 + g * 2 + e, 32, stride=16), :] = a_recv[
                        ex, g, e, t * 32 : t * 32 + 32, :
                    ].astype(F32)
            b_send[ex, t] = mix[t * 512 : t * 512 + 512, :].astype(BF)
            mine = pl.multiple_of(gb * 16, 16)

            def go_b(k):
                g = (gb + k) % 32
                rows = pl.ds(pl.multiple_of(g * 16, 16), 16)
                copy(
                    b_send.at[ex, t, rows], b_recv.at[ex, t, pl.ds(mine, 16)], b_sem.at[ex, t], peer_b(g)
                ).start()

            loop(1, 32, go_b)
            b_recv[ex, t, pl.ds(mine, 16)] = b_send[ex, t, pl.ds(mine, 16)]

    def wait_b(ex, t):
        part = b_recv.at[ex, t, pl.ds(0, 496)]
        copy(part, part, b_sem.at[ex, t], (rd, c)).wait_recv()

    def rows_0(e):
        copy(zr.at[e], zr.at[e], in_sem.at[e], (rd, c)).wait_recv()
        grid[...] = attend(zr[e], 0, 0)
        send_a(0, e, True)

    loop(0, 2, rows_0)
    send_b(0)

    def columns_0(t):
        wait_b(0, t)
        grid[...] = attend(b_recv[0, t], 0, 1)
        zc[t] = grid[...].astype(BF)
        send_a(1, t, False)

    loop(0, 2, columns_0)
    send_b(1)

    def rows_1(e):
        wait_b(1, e)
        symmetric = (0.5 * (zc[e].astype(F32) + b_recv[1, e].astype(F32))).astype(BF)
        grid[...] = attend(transition(symmetric.astype(F32), 0), 1, 0)
        send_a(2, e, False)

    loop(0, 2, rows_1)
    send_b(2)

    spot = pl.multiple_of((cy * 8 + zh * 4 + cx) * 16, 16)

    def columns_1(t):
        wait_b(2, t)
        grid[...] = attend(b_recv[2, t], 1, 1)
        for s in range(8):
            for e in range(2):
                part = grid[pl.ds((s // 2) * 128 + (s % 2) * 2 + e, 32, stride=4), :]
                a_send[3, s, t, e * 32 : e * 32 + 32, :] = part.astype(BF)
                mix[pl.ds(s * 2 + e, 32, stride=16), :] = part

        def go_t(k):
            s = (r + k) % 8
            copy(a_send.at[3, s, t], a_recv.at[3, rd, t], t_sem.at[t], (s, c)).start()

        loop(1, 8, go_t)
        a_recv[3, rd, t] = a_send[3, r, t]
        b_send[3, t] = mix[0:512, :].astype(BF)

        def go_m(k):
            w = (c + k) % 32
            rows = pl.ds(pl.multiple_of(((w // 8) * 8 + (w % 2) * 4 + (w // 2) % 4) * 16, 16), 16)
            copy(b_send.at[3, t, rows], b_recv.at[3, t, pl.ds(spot, 16)], m_sem.at[t], (rd, w)).start()

        loop(0, 32, go_m)

    loop(0, 2, columns_1)

    for t in range(2):
        part = a_recv.at[3, pl.ds(0, 7), t]
        copy(part, part, t_sem.at[t], (rd, c)).wait_recv()
    for e in range(2):
        for s in range(8):
            for t in range(2):
                mix[pl.ds(e * 512 + s * 2 + t, 32, stride=16), :] = a_recv[
                    3, s, t, e * 32 : e * 32 + 32, :
                ].astype(F32)
        copy(b_recv.at[3, e], b_recv.at[3, e], m_sem.at[e], (rd, c)).wait_recv()
        symmetric = (0.5 * (mix[e * 512 : e * 512 + 512, :] + b_recv[3, e].astype(F32))).astype(BF)
        final = transition(symmetric.astype(F32), 1)
        for y in range(4):
            for h in range(2):
                for q in range(4):
                    block = (y * 8 + h * 4 + q) * 16
                    out[y * 8 + q * 2 + h, e] = final[block : block + 16]

    for e in range(2):
        copy(zr.at[e], zr.at[e], in_sem.at[e], (rd, c)).wait_send()
        copy(b_recv.at[3, e], b_recv.at[3, e], m_sem.at[e], (rd, c)).wait_send()
        for ex in range(4):
            part = a_send.at[ex, pl.ds(0, 7), e]
            copy(part, part, t_sem.at[e], (rd, c)).wait_send()
        for ex in range(3):
            part = b_send.at[ex, e, pl.ds(0, 496)]
            copy(part, part, t_sem.at[e], (rd, c)).wait_send()


def local(pair, *weights):
    vmem = pltpu.VMEM
    dma = pltpu.SemaphoreType.DMA
    tile = pair.reshape(32, 2, 16, CHANNELS)
    result = pl.pallas_call(
        kernel,
        out_shape=jax.ShapeDtypeStruct(tile.shape, BF),
        in_specs=[pl.BlockSpec(memory_space=vmem)] * 8,
        out_specs=pl.BlockSpec(memory_space=vmem),
        scratch_shapes=[
            vmem((2, 2, INNER, CHANNELS), BF),
            vmem((2, 2, INNER, CHANNELS), BF),
            vmem((2, 2, INNER, CHANNELS), BF),
            vmem((INNER, LENGTH), BF),
            vmem((LENGTH, INNER), BF),
            vmem((HEADS, 48, LENGTH), BF),
            vmem((INNER, LENGTH), F32),
            vmem((INNER, LENGTH), BF),
            vmem((LENGTH, CHANNELS), F32),
            vmem((2 * LENGTH, CHANNELS), F32),
            vmem((2, LENGTH, CHANNELS), BF),
            vmem((2, LENGTH, CHANNELS), BF),
            vmem((4, 8, 2, 64, CHANNELS), BF),
            vmem((4, 8, 2, 64, CHANNELS), BF),
            vmem((4, 2, LENGTH, CHANNELS), BF),
            vmem((4, 2, LENGTH, CHANNELS), BF),
            dma,
            dma((2,)),
            dma((3, 2)),
            dma((3, 2)),
            dma((2,)),
            dma((2,)),
        ],
        compiler_params=pltpu.CompilerParams(
            collective_id=0, has_side_effects=True, vmem_limit_bytes=48 << 20
        ),
    )(tile, *weights)
    return result.reshape(pair.shape)


def solution(mesh):
    return jax.shard_map(
        local,
        mesh=mesh,
        in_specs=(P(None, "row", None, "col", None), P(), P(), P(), P(), P(), P(), P()),
        out_specs=P(None, "row", None, "col", None),
        check_vma=False,
    )
```

```python
import math

import jax
import jax.numpy as jnp
from jax import lax
from jax.experimental import pallas as pl
from jax.experimental.pallas import tpu as pltpu
from jax.sharding import PartitionSpec as P

HEADS = 8
HEAD_DIM = 32
INNER = HEADS * HEAD_DIM
CHANNELS = 128
LENGTH = 512
EPSILON = 1e-05
SCALE = math.log2(math.e) / math.sqrt(HEAD_DIM)
MESH = pl.DeviceIdType.MESH
BF = jnp.bfloat16
F32 = jnp.float32
NT = (((1,), (1,)), ((), ()))
TN = (((0,), (0,)), ((), ()))


def layer_norm(wide):
    center = wide - jnp.mean(wide, axis=-1, keepdims=True)
    spread = jnp.mean(center * center, axis=-1, keepdims=True)
    return (center * lax.rsqrt(spread + EPSILON)).astype(BF)


def kernel(
    x, hbm_query, hbm_key, hbm_value, hbm_gate, hbm_out, hbm_in, hbm_back, out,
    w_query, w_key, w_value, w_gate, w_out, w_in, w_back,
    wqt, wvt, wgt, qt, kr, vt, gt, go, grid, mix, stage,
    token, zcol, a_send, a_recv, b_send, inbox, t_send, t_recv, m_send, m_recv,
    send_sem, in_sem, a_sem, b_sem, t_sem, m_sem, w_sem,
):
    r = lax.axis_index("row")
    c = lax.axis_index("col")
    core = r % 2
    cy = c // 8
    cx = (c // 2) % 4
    zh = c % 2
    rd = (r + 4) % 8
    ga = cx * 2 + core
    gb = (rd // 2) * 8 + cy * 2 + zh

    def peer_a(g):
        return (r - core + g % 2, cy * 8 + (g // 2) * 2 + zh)

    def peer_b(g):
        return (((g // 8 + 2) % 4) * 2 + core, ((g // 2) % 4) * 8 + cx * 2 + g % 2)

    def copy(src, dst, sem, device):
        return pltpu.make_async_remote_copy(src, dst, send_sem, sem, device_id=device, device_id_type=MESH)

    def loop(start, stop, body):
        lax.fori_loop(start, stop, lambda k, carry: (body(k), carry)[1], 0)

    barrier = pltpu.get_barrier_semaphore()
    loop(0, 32, lambda k: pl.semaphore_signal(barrier, inc=1, device_id=(rd, k), device_id_type=MESH))
    loop(1, 8, lambda k: pl.semaphore_signal(barrier, inc=1, device_id=((r + k) % 8, c), device_id_type=MESH))
    fetches = [
        pltpu.make_async_copy(source, target, w_sem.at[i])
        for i, (source, target) in enumerate(
            (
                (hbm_query, w_query),
                (hbm_value, w_value),
                (hbm_gate, w_gate),
                (hbm_key, w_key),
                (hbm_out, w_out),
                (hbm_in, w_in),
                (hbm_back, w_back),
            )
        )
    ]
    for fetch in fetches:
        fetch.start()
    pl.semaphore_wait(barrier, 39)

    place = pl.multiple_of((cx * 8 + cy * 2 + zh) * 16, 16)
    for e in range(2):

        def send_rows(k):
            d = (c + k) % 32
            copy(x.at[d, e], inbox.at[0, e, pl.ds(place, 16)], in_sem.at[0, e], (rd, d)).start()

        loop(0, 32, send_rows)

    for fetch in fetches:
        fetch.wait()
    for l in range(2):
        for n in range(2):
            for source, target in ((w_query, wqt), (w_value, wvt), (w_gate, wgt)):
                target[l, n] = source[l, n].astype(F32).T.astype(BF)
    vt[...] = jnp.ones_like(vt)

    def project(l, n):
        normed = layer_norm(token[...])
        qt[...] = (lax.dot_general(wqt[l, n], normed, NT, preferred_element_type=F32) * SCALE).astype(BF)
        kr[...] = jnp.dot(normed, w_key[l, n], preferred_element_type=F32).astype(BF)
        value_rows = lax.dot_general(wvt[l, n], normed, NT, preferred_element_type=F32).astype(BF)
        for h in range(HEADS):
            vt[h, 0:HEAD_DIM, :] = value_rows[h * HEAD_DIM : (h + 1) * HEAD_DIM]
        gt[...] = jax.nn.sigmoid(lax.dot_general(wgt[l, n], normed, NT, preferred_element_type=F32))

    def attend(l, n, first, count):
        span = slice(first, first + count)

        def scores_of(h):
            rows = slice(h * HEAD_DIM, (h + 1) * HEAD_DIM)
            return jnp.dot(kr[:, rows], qt[rows, span], preferred_element_type=F32)

        def probs_of(scores):
            return jnp.exp2(scores - jnp.max(scores, axis=0, keepdims=True)).astype(BF)

        def blend(h, probs):
            rows = slice(h * HEAD_DIM, (h + 1) * HEAD_DIM)
            total = jnp.dot(vt[h], probs, preferred_element_type=F32)
            go[rows, span] = (gt[rows, span] * total[:HEAD_DIM] / total[HEAD_DIM : HEAD_DIM + 1]).astype(BF)

        scores = scores_of(0)
        probs = None
        for h in range(HEADS):
            later = scores_of(h + 1) if h + 1 < HEADS else None
            fresh = probs_of(scores)
            if probs is not None:
                blend(h - 1, probs)
            probs, scores = fresh, later
        blend(HEADS - 1, probs)
        update = lax.dot_general(go[:, span], w_out[l, n], TN, preferred_element_type=F32)
        grid[span, :] = token[span, :] + update

    def transition(wide, l):
        normed = layer_norm(wide)
        hidden = jax.nn.relu(jnp.dot(normed, w_in[l], preferred_element_type=F32)).astype(BF)
        return (wide + jnp.dot(hidden, w_back[l], preferred_element_type=F32)).astype(BF)

    def send_a(p, e, t):
        @pl.when(p == 0)
        def first_order():
            for g in range(8):
                for q in range(4):
                    start = t * 256 + (g // 2) * 64 + q * 2 + g % 2
                    stage[g * 32 + q * 8 : g * 32 + q * 8 + 8, :] = grid[pl.ds(start, 8, stride=8), :]

        @pl.when(p > 0)
        def later_order():
            for g in range(8):
                stage[g * 32 : g * 32 + 32, :] = grid[pl.ds(t * 256 + g, 32, stride=8), :]

        for g in range(8):
            a_send[p, e, t, g] = stage[g * 32 : g * 32 + 32, :].astype(BF)

        def go_a(k):
            g = (ga + k) % 8
            copy(a_send.at[p, e, t, g], a_recv.at[p, e, t, ga], a_sem.at[p, e, t], peer_a(g)).start()

        loop(1, 8, go_a)
        a_recv[p, e, t, ga] = a_send[p, e, t, ga]

    mine = pl.ds(pl.multiple_of(gb * 16, 16), 16)

    def send_b(p):
        for t in range(2):
            for e in range(2):
                part = a_recv.at[p, e, t, pl.ds(0, 7)]
                copy(part, part, a_sem.at[p, e, t], (rd, c)).wait_recv()
                for g in range(8):
                    mix[pl.ds(e * 8 + g, 32, stride=16), :] = a_recv[p, e, t, g].astype(F32)
            b_send[p, t] = mix[...].astype(BF)

            def go_b(k):
                g = (gb + k) % 32
                rows = pl.ds(pl.multiple_of(g * 16, 16), 16)
                copy(b_send.at[p, t, rows], inbox.at[p + 1, t, mine], b_sem.at[p, t], peer_b(g)).start()

            loop(1, 32, go_b)
            inbox[p + 1, t, mine] = b_send[p, t, mine]

    spot = pl.ds(place, 16)

    def send_tiles(t, e):
        for s in range(8):
            for q in range(4):
                start = e * 256 + (s // 2) * 64 + q * 2 + s % 2
                stage[s * 32 + q * 8 : s * 32 + q * 8 + 8, :] = grid[pl.ds(start, 8, stride=8), :]
        for s in range(8):
            t_send[e, t, s] = stage[s * 32 : s * 32 + 32, :].astype(BF)

        def go_t(k):
            s = (r + k) % 8
            copy(t_send.at[e, t, s], t_recv.at[e, t, rd], t_sem.at[e, t], (s, c)).start()

        loop(1, 8, go_t)
        t_recv[e, t, rd] = t_send[e, t, r]
        for s in range(8):
            mix[pl.ds(s * 2 + e, 32, stride=16), :] = stage[s * 32 : s * 32 + 32, :]

    def send_mirrored(t):
        m_send[t] = mix[...].astype(BF)

        def go_m(k):
            w = (c + k) % 32
            rows = pl.ds(pl.multiple_of((((w // 2) % 4) * 8 + (w // 8) * 2 + w % 2) * 16, 16), 16)
            copy(m_send.at[t, rows], m_recv.at[t, spot], m_sem.at[t], (rd, w)).start()

        loop(0, 32, go_m)

    def step(k):
        p = k // 2
        e = k % 2

        @pl.when(p == 0)
        def first_input():
            copy(inbox.at[0, e], inbox.at[0, e], in_sem.at[0, e], (rd, c)).wait_recv()
            mix[...] = inbox[0, e].astype(F32)
            for t in range(2):
                token[t * 256 : t * 256 + 256, :] = mix[pl.ds(t, 256, stride=2), :]

        @pl.when(p > 0)
        def later_input():
            part = inbox.at[p, e, pl.ds(0, 496)]
            copy(part, part, b_sem.at[p - 1, e], (rd, c)).wait_recv()
            for g in range(32):
                block = inbox[p, e, g * 16 : g * 16 + 16, :].astype(F32)
                for t in range(2):
                    token[t * 256 + g * 8 : t * 256 + g * 8 + 8, :] = block[t * 8 : t * 8 + 8]

        @pl.when(p == 2)
        def symmetrize():
            symmetric = (0.5 * (zcol[e].astype(F32) + token[...])).astype(BF)
            token[...] = transition(symmetric.astype(F32), 0).astype(F32)

        l = p // 2
        n = p % 2
        project(l, n)

        def send(t):
            @pl.when(p < 3)
            def exchange():
                send_a(p, e, t)

            @pl.when(p == 3)
            def finish():
                send_tiles(e, t)

        @pl.when(e == 0)
        def whole():
            attend(l, n, 0, 512)
            send(0)
            send(1)

        @pl.when(e == 1)
        def halves():
            attend(l, n, 0, 256)
            send(0)
            attend(l, n, 256, 256)
            send(1)

        @pl.when((p < 3) & (e == 1))
        def forward():
            send_b(p)

        @pl.when(p == 3)
        def mirror():
            send_mirrored(e)

        @pl.when(p == 1)
        def keep():
            zcol[e] = grid[...].astype(BF)

    loop(0, 8, step)

    def tile(e):
        for t in range(2):
            part = t_recv.at[e, t, pl.ds(0, 7)]
            copy(part, part, t_sem.at[e, t], (rd, c)).wait_recv()
            for s in range(8):
                mix[pl.ds(s * 2 + t, 32, stride=16), :] = t_recv[e, t, s].astype(F32)
        copy(m_recv.at[e], m_recv.at[e], m_sem.at[e], (rd, c)).wait_recv()
        symmetric = (0.5 * (mix[...] + m_recv[e].astype(F32))).astype(BF)
        final = transition(symmetric.astype(F32), 1)
        for q in range(4):
            for y in range(4):
                for h in range(2):
                    block = (q * 8 + y * 2 + h) * 16
                    out[y * 8 + q * 2 + h, e] = final[block : block + 16]

    loop(0, 2, tile)

    for e in range(2):
        copy(inbox.at[0, e], inbox.at[0, e], in_sem.at[0, e], (rd, c)).wait_send()
        copy(m_send.at[e], m_send.at[e], m_sem.at[e], (rd, c)).wait_send()
        for t in range(2):
            part = t_send.at[e, t, pl.ds(0, 7)]
            copy(part, part, in_sem.at[0, e], (rd, c)).wait_send()
        for p in range(3):
            for t in range(2):
                part = a_send.at[p, e, t, pl.ds(0, 7)]
                copy(part, part, in_sem.at[0, e], (rd, c)).wait_send()
            part = b_send.at[p, e, pl.ds(0, 496)]
            copy(part, part, in_sem.at[0, e], (rd, c)).wait_send()


def local(pair, *weights):
    vmem = pltpu.VMEM
    dma = pltpu.SemaphoreType.DMA
    tile = pair.reshape(32, 2, 16, CHANNELS)
    result = pl.pallas_call(
        kernel,
        out_shape=jax.ShapeDtypeStruct(tile.shape, BF),
        in_specs=[pl.BlockSpec(memory_space=pltpu.HBM)] * 8,
        out_specs=pl.BlockSpec(memory_space=vmem),
        scratch_shapes=[vmem(weight.shape, BF) for weight in weights]
        + [
            vmem((2, 2, INNER, CHANNELS), BF),
            vmem((2, 2, INNER, CHANNELS), BF),
            vmem((2, 2, INNER, CHANNELS), BF),
            vmem((INNER, LENGTH), BF),
            vmem((LENGTH, INNER), BF),
            vmem((HEADS, 48, LENGTH), BF),
            vmem((INNER, LENGTH), F32),
            vmem((INNER, LENGTH), BF),
            vmem((LENGTH, CHANNELS), F32),
            vmem((LENGTH, CHANNELS), F32),
            vmem((LENGTH, CHANNELS), F32),
            vmem((LENGTH, CHANNELS), F32),
            vmem((2, LENGTH, CHANNELS), BF),
            vmem((3, 2, 2, 8, 32, CHANNELS), BF),
            vmem((3, 2, 2, 8, 32, CHANNELS), BF),
            vmem((3, 2, LENGTH, CHANNELS), BF),
            vmem((4, 2, LENGTH, CHANNELS), BF),
            vmem((2, 2, 8, 32, CHANNELS), BF),
            vmem((2, 2, 8, 32, CHANNELS), BF),
            vmem((2, LENGTH, CHANNELS), BF),
            vmem((2, LENGTH, CHANNELS), BF),
            dma,
            dma((1, 2)),
            dma((3, 2, 2)),
            dma((3, 2)),
            dma((2, 2)),
            dma((2,)),
            dma((7,)),
        ],
        compiler_params=pltpu.CompilerParams(
            collective_id=0, has_side_effects=True, vmem_limit_bytes=62 << 20
        ),
    )(tile, *weights)
    return result.reshape(pair.shape)


def solution(mesh):
    return jax.shard_map(
        local,
        mesh=mesh,
        in_specs=(P(None, "row", None, "col", None), P(), P(), P(), P(), P(), P(), P()),
        out_specs=P(None, "row", None, "col", None),
        check_vma=False,
    )
```

```python
import math

import jax
import jax.numpy as jnp
from jax import lax
from jax.experimental import pallas as pl
from jax.experimental.pallas import tpu as pltpu
from jax.sharding import PartitionSpec as P

HEADS = 8
HEAD_DIM = 32
INNER = HEADS * HEAD_DIM
CHANNELS = 128
LENGTH = 512
EPSILON = 1e-05
SCALE = math.log2(math.e) / math.sqrt(HEAD_DIM)
MESH = pl.DeviceIdType.MESH
BF = jnp.bfloat16
F32 = jnp.float32
NT = (((1,), (1,)), ((), ()))
TN = (((0,), (0,)), ((), ()))


def layer_norm(wide):
    center = wide - jnp.mean(wide, axis=-1, keepdims=True)
    spread = jnp.mean(center * center, axis=-1, keepdims=True)
    return (center * lax.rsqrt(spread + EPSILON)).astype(BF)


def kernel(
    x, hbm_query, hbm_key, hbm_value, hbm_gate, hbm_out, hbm_in, hbm_back, out,
    w_query, w_key, w_value, w_gate, w_out, w_in, w_back,
    wqt, wvt, wgt, qt, kr, vt, gt, go, grid, mix, stage,
    token, zcol, a_send, a_recv, b_send, inbox, t_send, t_recv, m_send, m_recv,
    send_sem, in_sem, a_sem, b_sem, t_sem, m_sem, w_sem,
):
    r = lax.axis_index("row")
    c = lax.axis_index("col")
    core = r % 2
    cy = c // 8
    cx = (c // 2) % 4
    zh = c % 2
    rd = (r + 4) % 8
    ga = cx * 2 + core
    gb = (rd // 2) * 8 + cy * 2 + zh

    def peer_a(g):
        return (r - core + g % 2, cy * 8 + (g // 2) * 2 + zh)

    def peer_b(g):
        return (((g // 8 + 2) % 4) * 2 + core, ((g // 2) % 4) * 8 + cx * 2 + g % 2)

    def copy(src, dst, sem, device):
        return pltpu.make_async_remote_copy(src, dst, send_sem, sem, device_id=device, device_id_type=MESH)

    def loop(start, stop, body):
        lax.fori_loop(start, stop, lambda k, carry: (body(k), carry)[1], 0)

    barrier = pltpu.get_barrier_semaphore()
    loop(0, 32, lambda k: pl.semaphore_signal(barrier, inc=1, device_id=(rd, k), device_id_type=MESH))
    loop(1, 8, lambda k: pl.semaphore_signal(barrier, inc=1, device_id=((r + k) % 8, c), device_id_type=MESH))
    fetches = [
        pltpu.make_async_copy(source, target, w_sem.at[i])
        for i, (source, target) in enumerate(
            (
                (hbm_query, w_query),
                (hbm_value, w_value),
                (hbm_gate, w_gate),
                (hbm_key, w_key),
                (hbm_out, w_out),
                (hbm_in, w_in),
                (hbm_back, w_back),
            )
        )
    ]
    for fetch in fetches:
        fetch.start()
    pl.semaphore_wait(barrier, 39)

    place = pl.multiple_of((cx * 8 + cy * 2 + zh) * 16, 16)
    for e in range(2):

        def send_rows(k):
            d = (c + k) % 32
            copy(x.at[d, e], inbox.at[0, e, pl.ds(place, 16)], in_sem.at[0, e], (rd, d)).start()

        loop(0, 32, send_rows)

    for fetch in fetches:
        fetch.wait()
    for l in range(2):
        for n in range(2):
            for source, target in ((w_query, wqt), (w_value, wvt), (w_gate, wgt)):
                target[l, n] = source[l, n].astype(F32).T.astype(BF)
    vt[...] = jnp.ones_like(vt)

    def project(l, n):
        normed = layer_norm(token[...])
        qt[...] = (lax.dot_general(wqt[l, n], normed, NT, preferred_element_type=F32) * SCALE).astype(BF)
        kr[...] = jnp.dot(normed, w_key[l, n], preferred_element_type=F32).astype(BF)
        value_rows = lax.dot_general(wvt[l, n], normed, NT, preferred_element_type=F32).astype(BF)
        for h in range(HEADS):
            vt[h, 0:HEAD_DIM, :] = value_rows[h * HEAD_DIM : (h + 1) * HEAD_DIM]
        gt[...] = jax.nn.sigmoid(lax.dot_general(wgt[l, n], normed, NT, preferred_element_type=F32))

    def attend(l, n, first, count):
        span = slice(first, first + count)

        def scores_of(h):
            rows = slice(h * HEAD_DIM, (h + 1) * HEAD_DIM)
            return jnp.dot(kr[:, rows], qt[rows, span], preferred_element_type=F32)

        def probs_of(scores):
            return jnp.exp2(scores - jnp.max(scores, axis=0, keepdims=True)).astype(BF)

        def blend(h, probs):
            rows = slice(h * HEAD_DIM, (h + 1) * HEAD_DIM)
            total = jnp.dot(vt[h], probs, preferred_element_type=F32)
            inverse = 1.0 / total[HEAD_DIM : HEAD_DIM + 1]
            go[rows, span] = (gt[rows, span] * (total[:HEAD_DIM] * inverse)).astype(BF)

        scores = scores_of(0)
        probs = None
        for h in range(HEADS):
            later = scores_of(h + 1) if h + 1 < HEADS else None
            fresh = probs_of(scores)
            if probs is not None:
                blend(h - 1, probs)
            probs, scores = fresh, later
        blend(HEADS - 1, probs)
        update = lax.dot_general(go[:, span], w_out[l, n], TN, preferred_element_type=F32)
        grid[span, :] = token[span, :] + update

    def transition(wide, l):
        normed = layer_norm(wide)
        hidden = jax.nn.relu(jnp.dot(normed, w_in[l], preferred_element_type=F32)).astype(BF)
        return (wide + jnp.dot(hidden, w_back[l], preferred_element_type=F32)).astype(BF)

    def send_a(p, e, t):
        @pl.when(p == 0)
        def first_order():
            for g in range(8):
                for q in range(4):
                    start = t * 256 + (g // 2) * 64 + q * 2 + g % 2
                    stage[g * 32 + q * 8 : g * 32 + q * 8 + 8, :] = grid[pl.ds(start, 8, stride=8), :]

        @pl.when(p > 0)
        def later_order():
            for g in range(8):
                stage[g * 32 : g * 32 + 32, :] = grid[pl.ds(t * 256 + g, 32, stride=8), :]

        for g in range(8):
            a_send[p, e, t, g] = stage[g * 32 : g * 32 + 32, :].astype(BF)

        def go_a(k):
            g = (ga + k) % 8
            copy(a_send.at[p, e, t, g], a_recv.at[p, e, t, ga], a_sem.at[p, e, t], peer_a(g)).start()

        loop(1, 8, go_a)
        a_recv[p, e, t, ga] = a_send[p, e, t, ga]

    mine = pl.ds(pl.multiple_of(gb * 16, 16), 16)

    def build_b(p, t):
        for e in range(2):
            part = a_recv.at[p, e, t, pl.ds(0, 7)]
            copy(part, part, a_sem.at[p, e, t], (rd, c)).wait_recv()
            for g in range(8):
                mix[pl.ds(e * 8 + g, 32, stride=16), :] = a_recv[p, e, t, g].astype(F32)
        b_send[p, t] = mix[...].astype(BF)
        inbox[p + 1, t, mine] = b_send[p, t, mine]

    def start_b(p, t):
        def go_b(k):
            g = (gb + k) % 32
            rows = pl.ds(pl.multiple_of(g * 16, 16), 16)
            copy(b_send.at[p, t, rows], inbox.at[p + 1, t, mine], b_sem.at[p, t], peer_b(g)).start()

        loop(1, 32, go_b)

    spot = pl.ds(place, 16)

    def send_tiles(t, e):
        for s in range(8):
            for q in range(4):
                start = e * 256 + (s // 2) * 64 + q * 2 + s % 2
                stage[s * 32 + q * 8 : s * 32 + q * 8 + 8, :] = grid[pl.ds(start, 8, stride=8), :]
        for s in range(8):
            t_send[e, t, s] = stage[s * 32 : s * 32 + 32, :].astype(BF)

        def go_t(k):
            s = (r + k) % 8
            copy(t_send.at[e, t, s], t_recv.at[e, t, rd], t_sem.at[e, t], (s, c)).start()

        loop(1, 8, go_t)
        t_recv[e, t, rd] = t_send[e, t, r]
        for s in range(8):
            mix[pl.ds(s * 2 + e, 32, stride=16), :] = stage[s * 32 : s * 32 + 32, :]

    def send_mirrored(t):
        m_send[t] = mix[...].astype(BF)

        def go_m(k):
            w = (c + k) % 32
            rows = pl.ds(pl.multiple_of((((w // 2) % 4) * 8 + (w // 8) * 2 + w % 2) * 16, 16), 16)
            copy(m_send.at[t, rows], m_recv.at[t, spot], m_sem.at[t], (rd, w)).start()

        loop(0, 32, go_m)

    def step(k):
        p = k // 2
        e = k % 2

        @pl.when(p == 0)
        def first_input():
            copy(inbox.at[0, e], inbox.at[0, e], in_sem.at[0, e], (rd, c)).wait_recv()
            mix[...] = inbox[0, e].astype(F32)
            for t in range(2):
                token[t * 256 : t * 256 + 256, :] = mix[pl.ds(t, 256, stride=2), :]

        @pl.when(p > 0)
        def later_input():
            part = inbox.at[p, e, pl.ds(0, 496)]
            copy(part, part, b_sem.at[p - 1, e], (rd, c)).wait_recv()

            @pl.when(e == 0)
            def second():
                start_b(p - 1, 1)

            for g in range(32):
                block = inbox[p, e, g * 16 : g * 16 + 16, :].astype(F32)
                for t in range(2):
                    token[t * 256 + g * 8 : t * 256 + g * 8 + 8, :] = block[t * 8 : t * 8 + 8]

        @pl.when(p == 2)
        def symmetrize():
            symmetric = (0.5 * (zcol[e].astype(F32) + token[...])).astype(BF)
            token[...] = transition(symmetric.astype(F32), 0).astype(F32)

        l = p // 2
        n = p % 2
        project(l, n)

        def send(t):
            @pl.when(p < 3)
            def exchange():
                send_a(p, e, t)

            @pl.when(p == 3)
            def finish():
                send_tiles(e, t)

        @pl.when(e == 0)
        def whole():
            attend(l, n, 0, 512)
            send(0)
            send(1)

        @pl.when(e == 1)
        def halves():
            attend(l, n, 0, 256)
            send(0)
            attend(l, n, 256, 256)
            send(1)

        @pl.when((p < 3) & (e == 1))
        def forward():
            build_b(p, 0)
            start_b(p, 0)
            build_b(p, 1)

        @pl.when(p == 3)
        def mirror():
            send_mirrored(e)

        @pl.when(p == 1)
        def keep():
            zcol[e] = grid[...].astype(BF)

    loop(0, 8, step)

    def tile(e):
        for t in range(2):
            part = t_recv.at[e, t, pl.ds(0, 7)]
            copy(part, part, t_sem.at[e, t], (rd, c)).wait_recv()
            for s in range(8):
                mix[pl.ds(s * 2 + t, 32, stride=16), :] = t_recv[e, t, s].astype(F32)
        copy(m_recv.at[e], m_recv.at[e], m_sem.at[e], (rd, c)).wait_recv()
        symmetric = (0.5 * (mix[...] + m_recv[e].astype(F32))).astype(BF)
        final = transition(symmetric.astype(F32), 1)
        for q in range(4):
            for y in range(4):
                for h in range(2):
                    block = (q * 8 + y * 2 + h) * 16
                    out[y * 8 + q * 2 + h, e] = final[block : block + 16]

    loop(0, 2, tile)

    for e in range(2):
        copy(inbox.at[0, e], inbox.at[0, e], in_sem.at[0, e], (rd, c)).wait_send()
        copy(m_send.at[e], m_send.at[e], m_sem.at[e], (rd, c)).wait_send()
        for t in range(2):
            part = t_send.at[e, t, pl.ds(0, 7)]
            copy(part, part, in_sem.at[0, e], (rd, c)).wait_send()
        for p in range(3):
            for t in range(2):
                part = a_send.at[p, e, t, pl.ds(0, 7)]
                copy(part, part, in_sem.at[0, e], (rd, c)).wait_send()
            part = b_send.at[p, e, pl.ds(0, 496)]
            copy(part, part, in_sem.at[0, e], (rd, c)).wait_send()


def local(pair, *weights):
    vmem = pltpu.VMEM
    dma = pltpu.SemaphoreType.DMA
    tile = pair.reshape(32, 2, 16, CHANNELS)
    result = pl.pallas_call(
        kernel,
        out_shape=jax.ShapeDtypeStruct(tile.shape, BF),
        in_specs=[pl.BlockSpec(memory_space=pltpu.HBM)] * 8,
        out_specs=pl.BlockSpec(memory_space=vmem),
        scratch_shapes=[vmem(weight.shape, BF) for weight in weights]
        + [
            vmem((2, 2, INNER, CHANNELS), BF),
            vmem((2, 2, INNER, CHANNELS), BF),
            vmem((2, 2, INNER, CHANNELS), BF),
            vmem((INNER, LENGTH), BF),
            vmem((LENGTH, INNER), BF),
            vmem((HEADS, 48, LENGTH), BF),
            vmem((INNER, LENGTH), F32),
            vmem((INNER, LENGTH), BF),
            vmem((LENGTH, CHANNELS), F32),
            vmem((LENGTH, CHANNELS), F32),
            vmem((LENGTH, CHANNELS), F32),
            vmem((LENGTH, CHANNELS), F32),
            vmem((2, LENGTH, CHANNELS), BF),
            vmem((3, 2, 2, 8, 32, CHANNELS), BF),
            vmem((3, 2, 2, 8, 32, CHANNELS), BF),
            vmem((3, 2, LENGTH, CHANNELS), BF),
            vmem((4, 2, LENGTH, CHANNELS), BF),
            vmem((2, 2, 8, 32, CHANNELS), BF),
            vmem((2, 2, 8, 32, CHANNELS), BF),
            vmem((2, LENGTH, CHANNELS), BF),
            vmem((2, LENGTH, CHANNELS), BF),
            dma,
            dma((1, 2)),
            dma((3, 2, 2)),
            dma((3, 2)),
            dma((2, 2)),
            dma((2,)),
            dma((7,)),
        ],
        compiler_params=pltpu.CompilerParams(
            collective_id=0, has_side_effects=True, vmem_limit_bytes=62 << 20
        ),
    )(tile, *weights)
    return result.reshape(pair.shape)


def solution(mesh):
    return jax.shard_map(
        local,
        mesh=mesh,
        in_specs=(P(None, "row", None, "col", None), P(), P(), P(), P(), P(), P(), P()),
        out_specs=P(None, "row", None, "col", None),
        check_vma=False,
    )
```

```python
import math

import jax
import jax.numpy as jnp
from jax import lax
from jax.experimental import pallas as pl
from jax.experimental.pallas import tpu as pltpu
from jax.sharding import PartitionSpec as P

HEADS = 8
HEAD_DIM = 32
INNER = HEADS * HEAD_DIM
CHANNELS = 128
LENGTH = 512
EPSILON = 1e-05
SCALE = math.log2(math.e) / math.sqrt(HEAD_DIM)
MESH = pl.DeviceIdType.MESH
BF = jnp.bfloat16
F32 = jnp.float32
NT = (((1,), (1,)), ((), ()))
TN = (((0,), (0,)), ((), ()))


def layer_norm(wide):
    center = wide - jnp.mean(wide, axis=-1, keepdims=True)
    spread = jnp.mean(center * center, axis=-1, keepdims=True)
    return (center * lax.rsqrt(spread + EPSILON)).astype(BF)


def kernel(
    x, hbm_query, hbm_key, hbm_value, hbm_gate, hbm_out, hbm_in, hbm_back, out,
    w_query, w_key, w_value, w_gate, w_out, w_in, w_back,
    wqt, wvt, wgt, qt, kr, vt, gt, go, grid, mix, stage,
    token, zcol, a_send, a_recv, b_send, inbox, t_send, t_recv, m_send, m_recv,
    send_sem, in_sem, a_sem, b_sem, t_sem, m_sem, w_sem,
):
    r = lax.axis_index("row")
    c = lax.axis_index("col")
    core = r % 2
    cy = c // 8
    cx = (c // 2) % 4
    zh = c % 2
    rd = (r + 4) % 8
    ga = cx * 2 + core
    gb = (rd // 2) * 8 + cy * 2 + zh

    def peer_a(g):
        return (r - core + g % 2, cy * 8 + (g // 2) * 2 + zh)

    def peer_b(g):
        return (((g // 8 + 2) % 4) * 2 + core, ((g // 2) % 4) * 8 + cx * 2 + g % 2)

    def copy(src, dst, sem, device):
        return pltpu.make_async_remote_copy(src, dst, send_sem, sem, device_id=device, device_id_type=MESH)

    def loop(start, stop, body):
        lax.fori_loop(start, stop, lambda k, carry: (body(k), carry)[1], 0)

    barrier = pltpu.get_barrier_semaphore()
    loop(0, 32, lambda k: pl.semaphore_signal(barrier, inc=1, device_id=(rd, k), device_id_type=MESH))
    loop(1, 8, lambda k: pl.semaphore_signal(barrier, inc=1, device_id=((r + k) % 8, c), device_id_type=MESH))
    fetches = [
        pltpu.make_async_copy(source, target, w_sem.at[i])
        for i, (source, target) in enumerate(
            (
                (hbm_query, w_query),
                (hbm_value, w_value),
                (hbm_gate, w_gate),
                (hbm_key, w_key),
                (hbm_out, w_out),
                (hbm_in, w_in),
                (hbm_back, w_back),
            )
        )
    ]
    for fetch in fetches:
        fetch.start()
    pl.semaphore_wait(barrier, 39)

    place = pl.multiple_of((cx * 8 + cy * 2 + zh) * 16, 16)
    for e in range(2):

        def send_rows(k):
            d = (c + k) % 32
            copy(x.at[d, e], inbox.at[0, e, pl.ds(place, 16)], in_sem.at[0, e], (rd, d)).start()

        loop(0, 32, send_rows)

    for fetch in fetches:
        fetch.wait()
    for l in range(2):
        for n in range(2):
            for source, target in ((w_query, wqt), (w_value, wvt), (w_gate, wgt)):
                target[l, n] = source[l, n].astype(F32).T.astype(BF)
    vt[...] = jnp.ones_like(vt)

    def project(l, n):
        normed = layer_norm(token[...])
        qt[...] = (lax.dot_general(wqt[l, n], normed, NT, preferred_element_type=F32) * SCALE).astype(BF)
        kr[...] = jnp.dot(normed, w_key[l, n], preferred_element_type=F32).astype(BF)
        value_rows = lax.dot_general(wvt[l, n], normed, NT, preferred_element_type=F32).astype(BF)
        for h in range(HEADS):
            vt[h, 0:HEAD_DIM, :] = value_rows[h * HEAD_DIM : (h + 1) * HEAD_DIM]
        gt[...] = jax.nn.sigmoid(lax.dot_general(wgt[l, n], normed, NT, preferred_element_type=F32))

    def attend(l, n, first, count):
        span = slice(first, first + count)

        def scores_of(h):
            rows = slice(h * HEAD_DIM, (h + 1) * HEAD_DIM)
            return jnp.dot(kr[:, rows], qt[rows, span], preferred_element_type=F32)

        def probs_of(scores):
            return jnp.exp2(scores - jnp.max(scores, axis=0, keepdims=True)).astype(BF)

        def blend(h, probs):
            rows = slice(h * HEAD_DIM, (h + 1) * HEAD_DIM)
            total = jnp.dot(vt[h], probs, preferred_element_type=F32)
            inverse = 1.0 / total[HEAD_DIM : HEAD_DIM + 1]
            go[rows, span] = (gt[rows, span] * (total[:HEAD_DIM] * inverse)).astype(BF)

        scores = scores_of(0)
        probs = None
        for h in range(HEADS):
            later = scores_of(h + 1) if h + 1 < HEADS else None
            fresh = probs_of(scores)
            if probs is not None:
                blend(h - 1, probs)
            probs, scores = fresh, later
        blend(HEADS - 1, probs)
        update = lax.dot_general(go[:, span], w_out[l, n], TN, preferred_element_type=F32)
        grid[span, :] = token[span, :] + update

    def transition(wide, l):
        normed = layer_norm(wide)
        hidden = jax.nn.relu(jnp.dot(normed, w_in[l], preferred_element_type=F32)).astype(BF)
        return (wide + jnp.dot(hidden, w_back[l], preferred_element_type=F32)).astype(BF)

    def send_a(p, e, t):
        @pl.when(p == 0)
        def first_order():
            for g in range(8):
                for q in range(4):
                    start = t * 256 + (g // 2) * 64 + q * 2 + g % 2
                    stage[g * 32 + q * 8 : g * 32 + q * 8 + 8, :] = grid[pl.ds(start, 8, stride=8), :]

        @pl.when(p > 0)
        def later_order():
            for g in range(8):
                stage[g * 32 : g * 32 + 32, :] = grid[pl.ds(t * 256 + g, 32, stride=8), :]

        for g in range(8):
            a_send[p, e, t, g] = stage[g * 32 : g * 32 + 32, :].astype(BF)

        def go_a(k):
            g = (ga + k) % 8
            copy(a_send.at[p, e, t, g], a_recv.at[p, e, t, ga], a_sem.at[p, e, t], peer_a(g)).start()

        loop(1, 8, go_a)
        a_recv[p, e, t, ga] = a_send[p, e, t, ga]

    mine = pl.ds(pl.multiple_of(gb * 16, 16), 16)

    def send_b(p):
        for t in range(2):
            for e in range(2):
                part = a_recv.at[p, e, t, pl.ds(0, 7)]
                copy(part, part, a_sem.at[p, e, t], (rd, c)).wait_recv()
                for g in range(8):
                    mix[pl.ds(e * 8 + g, 32, stride=16), :] = a_recv[p, e, t, g].astype(F32)
            b_send[p, t] = mix[...].astype(BF)

            def go_b(k):
                g = (gb + k) % 32
                rows = pl.ds(pl.multiple_of(g * 16, 16), 16)
                copy(b_send.at[p, t, rows], inbox.at[p + 1, t, mine], b_sem.at[p, t], peer_b(g)).start()

            loop(1, 32, go_b)
            inbox[p + 1, t, mine] = b_send[p, t, mine]

    spot = pl.ds(place, 16)

    def send_tiles(t, e):
        for s in range(8):
            for q in range(4):
                start = e * 256 + (s // 2) * 64 + q * 2 + s % 2
                stage[s * 32 + q * 8 : s * 32 + q * 8 + 8, :] = grid[pl.ds(start, 8, stride=8), :]
        for s in range(8):
            t_send[e, t, s] = stage[s * 32 : s * 32 + 32, :].astype(BF)

        def go_t(k):
            s = (r + k) % 8
            copy(t_send.at[e, t, s], t_recv.at[e, t, rd], t_sem.at[e, t], (s, c)).start()

        loop(1, 8, go_t)
        t_recv[e, t, rd] = t_send[e, t, r]
        for s in range(8):
            mix[pl.ds(s * 2 + e, 32, stride=16), :] = stage[s * 32 : s * 32 + 32, :]

    def send_mirrored(t):
        m_send[t] = mix[...].astype(BF)

        def go_m(k):
            w = (c + k) % 32
            rows = pl.ds(pl.multiple_of((((w // 2) % 4) * 8 + (w // 8) * 2 + w % 2) * 16, 16), 16)
            copy(m_send.at[t, rows], m_recv.at[t, spot], m_sem.at[t], (rd, w)).start()

        loop(0, 32, go_m)

    def step(k):
        p = k // 2
        e = k % 2

        @pl.when(p == 0)
        def first_input():
            copy(inbox.at[0, e], inbox.at[0, e], in_sem.at[0, e], (rd, c)).wait_recv()
            mix[...] = inbox[0, e].astype(F32)
            for t in range(2):
                token[t * 256 : t * 256 + 256, :] = mix[pl.ds(t, 256, stride=2), :]

        @pl.when(p > 0)
        def later_input():
            part = inbox.at[p, e, pl.ds(0, 496)]
            copy(part, part, b_sem.at[p - 1, e], (rd, c)).wait_recv()
            for g in range(32):
                block = inbox[p, e, g * 16 : g * 16 + 16, :].astype(F32)
                for t in range(2):
                    token[t * 256 + g * 8 : t * 256 + g * 8 + 8, :] = block[t * 8 : t * 8 + 8]

        @pl.when(p == 2)
        def symmetrize():
            symmetric = (0.5 * (zcol[e].astype(F32) + token[...])).astype(BF)
            token[...] = transition(symmetric.astype(F32), 0).astype(F32)

        l = p // 2
        n = p % 2
        project(l, n)

        def send(t):
            @pl.when(p < 3)
            def exchange():
                send_a(p, e, t)

            @pl.when(p == 3)
            def finish():
                send_tiles(e, t)

        @pl.when(e == 0)
        def whole():
            attend(l, n, 0, 512)
            send(0)
            send(1)

        @pl.when(e == 1)
        def halves():
            attend(l, n, 0, 256)
            send(0)
            attend(l, n, 256, 256)
            send(1)

        @pl.when((p < 3) & (e == 1))
        def forward():
            send_b(p)

        @pl.when(p == 3)
        def mirror():
            send_mirrored(e)

        @pl.when(p == 1)
        def keep():
            zcol[e] = grid[...].astype(BF)

    loop(0, 8, step)

    def tile(e):
        for t in range(2):
            part = t_recv.at[e, t, pl.ds(0, 7)]
            copy(part, part, t_sem.at[e, t], (rd, c)).wait_recv()
            for s in range(8):
                mix[pl.ds(s * 2 + t, 32, stride=16), :] = t_recv[e, t, s].astype(F32)
        copy(m_recv.at[e], m_recv.at[e], m_sem.at[e], (rd, c)).wait_recv()
        symmetric = (0.5 * (mix[...] + m_recv[e].astype(F32))).astype(BF)
        final = transition(symmetric.astype(F32), 1)
        for q in range(4):
            for y in range(4):
                for h in range(2):
                    block = (q * 8 + y * 2 + h) * 16
                    out[y * 8 + q * 2 + h, e] = final[block : block + 16]

    loop(0, 2, tile)

    for e in range(2):
        copy(inbox.at[0, e], inbox.at[0, e], in_sem.at[0, e], (rd, c)).wait_send()
        copy(m_send.at[e], m_send.at[e], m_sem.at[e], (rd, c)).wait_send()
        for t in range(2):
            part = t_send.at[e, t, pl.ds(0, 7)]
            copy(part, part, in_sem.at[0, e], (rd, c)).wait_send()
        for p in range(3):
            for t in range(2):
                part = a_send.at[p, e, t, pl.ds(0, 7)]
                copy(part, part, in_sem.at[0, e], (rd, c)).wait_send()
            part = b_send.at[p, e, pl.ds(0, 496)]
            copy(part, part, in_sem.at[0, e], (rd, c)).wait_send()


def local(pair, *weights):
    vmem = pltpu.VMEM
    dma = pltpu.SemaphoreType.DMA
    tile = pair.reshape(32, 2, 16, CHANNELS)
    result = pl.pallas_call(
        kernel,
        out_shape=jax.ShapeDtypeStruct(tile.shape, BF),
        in_specs=[pl.BlockSpec(memory_space=pltpu.HBM)] * 8,
        out_specs=pl.BlockSpec(memory_space=vmem),
        scratch_shapes=[vmem(weight.shape, BF) for weight in weights]
        + [
            vmem((2, 2, INNER, CHANNELS), BF),
            vmem((2, 2, INNER, CHANNELS), BF),
            vmem((2, 2, INNER, CHANNELS), BF),
            vmem((INNER, LENGTH), BF),
            vmem((LENGTH, INNER), BF),
            vmem((HEADS, 48, LENGTH), BF),
            vmem((INNER, LENGTH), F32),
            vmem((INNER, LENGTH), BF),
            vmem((LENGTH, CHANNELS), F32),
            vmem((LENGTH, CHANNELS), F32),
            vmem((LENGTH, CHANNELS), F32),
            vmem((LENGTH, CHANNELS), F32),
            vmem((2, LENGTH, CHANNELS), BF),
            vmem((3, 2, 2, 8, 32, CHANNELS), BF),
            vmem((3, 2, 2, 8, 32, CHANNELS), BF),
            vmem((3, 2, LENGTH, CHANNELS), BF),
            vmem((4, 2, LENGTH, CHANNELS), BF),
            vmem((2, 2, 8, 32, CHANNELS), BF),
            vmem((2, 2, 8, 32, CHANNELS), BF),
            vmem((2, LENGTH, CHANNELS), BF),
            vmem((2, LENGTH, CHANNELS), BF),
            dma,
            dma((1, 2)),
            dma((3, 2, 2)),
            dma((3, 2)),
            dma((2, 2)),
            dma((2,)),
            dma((7,)),
        ],
        compiler_params=pltpu.CompilerParams(
            collective_id=0, has_side_effects=True, vmem_limit_bytes=62 << 20
        ),
    )(tile, *weights)
    return result.reshape(pair.shape)


def solution(mesh):
    return jax.shard_map(
        local,
        mesh=mesh,
        in_specs=(P(None, "row", None, "col", None), P(), P(), P(), P(), P(), P(), P()),
        out_specs=P(None, "row", None, "col", None),
        check_vma=False,
    )
```

```python
import math

import jax
import jax.numpy as jnp
from jax import lax
from jax.experimental import pallas as pl
from jax.experimental.pallas import tpu as pltpu
from jax.sharding import PartitionSpec as P

HEADS = 8
HEAD_DIM = 32
INNER = HEADS * HEAD_DIM
CHANNELS = 128
LENGTH = 512
EPSILON = 1e-05
SCALE = math.log2(math.e) / math.sqrt(HEAD_DIM)
MESH = pl.DeviceIdType.MESH
BF = jnp.bfloat16
F32 = jnp.float32
NT = (((1,), (1,)), ((), ()))
TN = (((0,), (0,)), ((), ()))


def layer_norm(wide):
    center = wide - jnp.mean(wide, axis=-1, keepdims=True)
    spread = jnp.mean(center * center, axis=-1, keepdims=True)
    return (center * lax.rsqrt(spread + EPSILON)).astype(BF)


def kernel(
    x, hbm_query, hbm_key, hbm_value, hbm_gate, hbm_out, hbm_in, hbm_back, out,
    w_query, w_key, w_value, w_gate, w_out, w_in, w_back,
    wqt, wvt, wgt, qt, kr, vt, gt, go, grid, mix, stage,
    token, zcol, a_send, a_recv, b_send, inbox, t_send, t_recv, m_send, m_recv,
    send_sem, in_sem, a_sem, b_sem, t_sem, m_sem, w_sem,
):
    r = lax.axis_index("row")
    c = lax.axis_index("col")
    core = r % 2
    cy = c // 8
    cx = (c // 2) % 4
    zh = c % 2
    rd = (r + 4) % 8
    ga = cx * 2 + core
    gb = (rd // 2) * 8 + cy * 2 + zh

    def peer_a(g):
        return (r - core + g % 2, cy * 8 + (g // 2) * 2 + zh)

    def peer_b(g):
        return (((g // 8 + 2) % 4) * 2 + core, ((g // 2) % 4) * 8 + cx * 2 + g % 2)

    def copy(src, dst, sem, device):
        return pltpu.make_async_remote_copy(src, dst, send_sem, sem, device_id=device, device_id_type=MESH)

    def loop(start, stop, body):
        lax.fori_loop(start, stop, lambda k, carry: (body(k), carry)[1], 0)

    barrier = pltpu.get_barrier_semaphore()
    loop(0, 32, lambda k: pl.semaphore_signal(barrier, inc=1, device_id=(rd, k), device_id_type=MESH))
    loop(1, 8, lambda k: pl.semaphore_signal(barrier, inc=1, device_id=((r + k) % 8, c), device_id_type=MESH))
    fetches = [
        pltpu.make_async_copy(source, target, w_sem.at[i])
        for i, (source, target) in enumerate(
            (
                (hbm_query, w_query),
                (hbm_value, w_value),
                (hbm_gate, w_gate),
                (hbm_key, w_key),
                (hbm_out, w_out),
                (hbm_in, w_in),
                (hbm_back, w_back),
            )
        )
    ]
    for fetch in fetches:
        fetch.start()
    pl.semaphore_wait(barrier, 39)

    place = pl.multiple_of((cx * 8 + cy * 2 + zh) * 16, 16)
    for e in range(2):

        def send_rows(k):
            d = (c + k * 13) % 32
            copy(x.at[d, e], inbox.at[0, e, pl.ds(place, 16)], in_sem.at[0, e], (rd, d)).start()

        loop(0, 32, send_rows)

    for fetch in fetches:
        fetch.wait()
    for l in range(2):
        for n in range(2):
            for source, target in ((w_query, wqt), (w_value, wvt), (w_gate, wgt)):
                target[l, n] = source[l, n].astype(F32).T.astype(BF)
    vt[...] = jnp.ones_like(vt)

    def project(l, n):
        normed = layer_norm(token[...])
        qt[...] = (lax.dot_general(wqt[l, n], normed, NT, preferred_element_type=F32) * SCALE).astype(BF)
        kr[...] = jnp.dot(normed, w_key[l, n], preferred_element_type=F32).astype(BF)
        value_rows = lax.dot_general(wvt[l, n], normed, NT, preferred_element_type=F32).astype(BF)
        for h in range(HEADS):
            vt[h, 0:HEAD_DIM, :] = value_rows[h * HEAD_DIM : (h + 1) * HEAD_DIM]
        gt[...] = jax.nn.sigmoid(lax.dot_general(wgt[l, n], normed, NT, preferred_element_type=F32))

    def attend(l, n, first, count):
        span = slice(first, first + count)

        def scores_of(h):
            rows = slice(h * HEAD_DIM, (h + 1) * HEAD_DIM)
            return jnp.dot(kr[:, rows], qt[rows, span], preferred_element_type=F32)

        def probs_of(scores):
            return jnp.exp2(scores - jnp.max(scores, axis=0, keepdims=True)).astype(BF)

        def blend(h, probs):
            rows = slice(h * HEAD_DIM, (h + 1) * HEAD_DIM)
            total = jnp.dot(vt[h], probs, preferred_element_type=F32)
            go[rows, span] = (gt[rows, span] * total[:HEAD_DIM] / total[HEAD_DIM : HEAD_DIM + 1]).astype(BF)

        scores = scores_of(0)
        probs = None
        for h in range(HEADS):
            later = scores_of(h + 1) if h + 1 < HEADS else None
            fresh = probs_of(scores)
            if probs is not None:
                blend(h - 1, probs)
            probs, scores = fresh, later
        blend(HEADS - 1, probs)
        update = lax.dot_general(go[:, span], w_out[l, n], TN, preferred_element_type=F32)
        grid[span, :] = token[span, :] + update

    def transition(wide, l):
        normed = layer_norm(wide)
        hidden = jax.nn.relu(jnp.dot(normed, w_in[l], preferred_element_type=F32)).astype(BF)
        return (wide + jnp.dot(hidden, w_back[l], preferred_element_type=F32)).astype(BF)

    def send_a(p, e, t):
        @pl.when(p == 0)
        def first_order():
            for g in range(8):
                for q in range(4):
                    start = t * 256 + (g // 2) * 64 + q * 2 + g % 2
                    stage[g * 32 + q * 8 : g * 32 + q * 8 + 8, :] = grid[pl.ds(start, 8, stride=8), :]

        @pl.when(p > 0)
        def later_order():
            for g in range(8):
                stage[g * 32 : g * 32 + 32, :] = grid[pl.ds(t * 256 + g, 32, stride=8), :]

        for g in range(8):
            a_send[p, e, t, g] = stage[g * 32 : g * 32 + 32, :].astype(BF)

        def go_a(k):
            g = (ga + k) % 8
            copy(a_send.at[p, e, t, g], a_recv.at[p, e, t, ga], a_sem.at[p, e, t], peer_a(g)).start()

        loop(1, 8, go_a)
        a_recv[p, e, t, ga] = a_send[p, e, t, ga]

    mine = pl.ds(pl.multiple_of(gb * 16, 16), 16)

    def send_b(p):
        for t in range(2):
            for e in range(2):
                part = a_recv.at[p, e, t, pl.ds(0, 7)]
                copy(part, part, a_sem.at[p, e, t], (rd, c)).wait_recv()
                for g in range(8):
                    mix[pl.ds(e * 8 + g, 32, stride=16), :] = a_recv[p, e, t, g].astype(F32)
            b_send[p, t] = mix[...].astype(BF)

            def go_b(k):
                g = (gb + k * 13) % 32
                rows = pl.ds(pl.multiple_of(g * 16, 16), 16)
                copy(b_send.at[p, t, rows], inbox.at[p + 1, t, mine], b_sem.at[p, t], peer_b(g)).start()

            loop(1, 32, go_b)
            inbox[p + 1, t, mine] = b_send[p, t, mine]

    spot = pl.ds(place, 16)

    def send_tiles(t, e):
        for s in range(8):
            for q in range(4):
                start = e * 256 + (s // 2) * 64 + q * 2 + s % 2
                stage[s * 32 + q * 8 : s * 32 + q * 8 + 8, :] = grid[pl.ds(start, 8, stride=8), :]
        for s in range(8):
            t_send[e, t, s] = stage[s * 32 : s * 32 + 32, :].astype(BF)

        def go_t(k):
            s = (r + k) % 8
            copy(t_send.at[e, t, s], t_recv.at[e, t, rd], t_sem.at[e, t], (s, c)).start()

        loop(1, 8, go_t)
        t_recv[e, t, rd] = t_send[e, t, r]
        for s in range(8):
            mix[pl.ds(s * 2 + e, 32, stride=16), :] = stage[s * 32 : s * 32 + 32, :]

    def send_mirrored(t):
        m_send[t] = mix[...].astype(BF)

        def go_m(k):
            w = (c + k * 13) % 32
            rows = pl.ds(pl.multiple_of((((w // 2) % 4) * 8 + (w // 8) * 2 + w % 2) * 16, 16), 16)
            copy(m_send.at[t, rows], m_recv.at[t, spot], m_sem.at[t], (rd, w)).start()

        loop(0, 32, go_m)

    def step(k):
        p = k // 2
        e = k % 2

        @pl.when(p == 0)
        def first_input():
            copy(inbox.at[0, e], inbox.at[0, e], in_sem.at[0, e], (rd, c)).wait_recv()
            mix[...] = inbox[0, e].astype(F32)
            for t in range(2):
                token[t * 256 : t * 256 + 256, :] = mix[pl.ds(t, 256, stride=2), :]

        @pl.when(p > 0)
        def later_input():
            part = inbox.at[p, e, pl.ds(0, 496)]
            copy(part, part, b_sem.at[p - 1, e], (rd, c)).wait_recv()
            for g in range(32):
                block = inbox[p, e, g * 16 : g * 16 + 16, :].astype(F32)
                for t in range(2):
                    token[t * 256 + g * 8 : t * 256 + g * 8 + 8, :] = block[t * 8 : t * 8 + 8]

        @pl.when(p == 2)
        def symmetrize():
            symmetric = (0.5 * (zcol[e].astype(F32) + token[...])).astype(BF)
            token[...] = transition(symmetric.astype(F32), 0).astype(F32)

        l = p // 2
        n = p % 2
        project(l, n)

        def send(t):
            @pl.when(p < 3)
            def exchange():
                send_a(p, e, t)

            @pl.when(p == 3)
            def finish():
                send_tiles(e, t)

        @pl.when(e == 0)
        def whole():
            attend(l, n, 0, 512)
            send(0)
            send(1)

        @pl.when(e == 1)
        def halves():
            attend(l, n, 0, 256)
            send(0)
            attend(l, n, 256, 256)
            send(1)

        @pl.when((p < 3) & (e == 1))
        def forward():
            send_b(p)

        @pl.when(p == 3)
        def mirror():
            send_mirrored(e)

        @pl.when(p == 1)
        def keep():
            zcol[e] = grid[...].astype(BF)

    loop(0, 8, step)

    def tile(e):
        for t in range(2):
            part = t_recv.at[e, t, pl.ds(0, 7)]
            copy(part, part, t_sem.at[e, t], (rd, c)).wait_recv()
            for s in range(8):
                mix[pl.ds(s * 2 + t, 32, stride=16), :] = t_recv[e, t, s].astype(F32)
        copy(m_recv.at[e], m_recv.at[e], m_sem.at[e], (rd, c)).wait_recv()
        symmetric = (0.5 * (mix[...] + m_recv[e].astype(F32))).astype(BF)
        final = transition(symmetric.astype(F32), 1)
        for q in range(4):
            for y in range(4):
                for h in range(2):
                    block = (q * 8 + y * 2 + h) * 16
                    out[y * 8 + q * 2 + h, e] = final[block : block + 16]

    loop(0, 2, tile)

    for e in range(2):
        copy(inbox.at[0, e], inbox.at[0, e], in_sem.at[0, e], (rd, c)).wait_send()
        copy(m_send.at[e], m_send.at[e], m_sem.at[e], (rd, c)).wait_send()
        for t in range(2):
            part = t_send.at[e, t, pl.ds(0, 7)]
            copy(part, part, in_sem.at[0, e], (rd, c)).wait_send()
        for p in range(3):
            for t in range(2):
                part = a_send.at[p, e, t, pl.ds(0, 7)]
                copy(part, part, in_sem.at[0, e], (rd, c)).wait_send()
            part = b_send.at[p, e, pl.ds(0, 496)]
            copy(part, part, in_sem.at[0, e], (rd, c)).wait_send()


def local(pair, *weights):
    vmem = pltpu.VMEM
    dma = pltpu.SemaphoreType.DMA
    tile = pair.reshape(32, 2, 16, CHANNELS)
    result = pl.pallas_call(
        kernel,
        out_shape=jax.ShapeDtypeStruct(tile.shape, BF),
        in_specs=[pl.BlockSpec(memory_space=pltpu.HBM)] * 8,
        out_specs=pl.BlockSpec(memory_space=vmem),
        scratch_shapes=[vmem(weight.shape, BF) for weight in weights]
        + [
            vmem((2, 2, INNER, CHANNELS), BF),
            vmem((2, 2, INNER, CHANNELS), BF),
            vmem((2, 2, INNER, CHANNELS), BF),
            vmem((INNER, LENGTH), BF),
            vmem((LENGTH, INNER), BF),
            vmem((HEADS, 48, LENGTH), BF),
            vmem((INNER, LENGTH), F32),
            vmem((INNER, LENGTH), BF),
            vmem((LENGTH, CHANNELS), F32),
            vmem((LENGTH, CHANNELS), F32),
            vmem((LENGTH, CHANNELS), F32),
            vmem((LENGTH, CHANNELS), F32),
            vmem((2, LENGTH, CHANNELS), BF),
            vmem((3, 2, 2, 8, 32, CHANNELS), BF),
            vmem((3, 2, 2, 8, 32, CHANNELS), BF),
            vmem((3, 2, LENGTH, CHANNELS), BF),
            vmem((4, 2, LENGTH, CHANNELS), BF),
            vmem((2, 2, 8, 32, CHANNELS), BF),
            vmem((2, 2, 8, 32, CHANNELS), BF),
            vmem((2, LENGTH, CHANNELS), BF),
            vmem((2, LENGTH, CHANNELS), BF),
            dma,
            dma((1, 2)),
            dma((3, 2, 2)),
            dma((3, 2)),
            dma((2, 2)),
            dma((2,)),
            dma((7,)),
        ],
        compiler_params=pltpu.CompilerParams(
            collective_id=0, has_side_effects=True, vmem_limit_bytes=62 << 20
        ),
    )(tile, *weights)
    return result.reshape(pair.shape)


def solution(mesh):
    return jax.shard_map(
        local,
        mesh=mesh,
        in_specs=(P(None, "row", None, "col", None), P(), P(), P(), P(), P(), P(), P()),
        out_specs=P(None, "row", None, "col", None),
        check_vma=False,
    )
```
